32 devices in a mesh: groups: 2 (over y), bank: 4 (over x, core), tensor: 4 (over z).
Axes of the slice: x: 2, y: 2, z: 4, core: 2. Of those that a mesh axis runs over, the one named last changes fastest.
Arguments:
- normed: bfloat16 [6144, 8192], P(('groups', 'bank'), 'tensor'), parts along dimension 0, may hold values from -6 to 6
- turn_persona_ids: int32 [384], P(('groups', 'bank')), parts along dimension 0, may hold values from 0 to 127, as said below
- persona_bank_row: int32 [256], P('groups'), parts along dimension 0, may hold values from 0 to 127, as said below
- key_weight: bfloat16 [8192, 1024], P('tensor'), may hold values from -0.0625 to 0.0625
- value_weight: bfloat16 [8192, 1024], P('tensor'), may hold values from -0.0625 to 0.0625
- adapter_down_factor: bfloat16 [256, 64, 8192], P(('groups', 'bank'), None, 'tensor'), parts along dimension 0, may hold values from -0.0625 to 0.0625
- adapter_up_factor: bfloat16 [256, 64, 1024], P(('groups', 'bank'), None, 'tensor'), parts along dimension 0, may hold values from -0.375 to 0.375
Outputs:
- keys: bfloat16 [6144, 1024], P(('groups', 'bank'), 'tensor'), parts along dimension 0
- values: bfloat16 [6144, 1024], P(('groups', 'bank'), 'tensor'), parts along dimension 0
The draws below stay inside these ranges and needn't reach their ends.
There are 2 independent parts, one for each index of `groups`. The reference program is written for one: setup_inputs(seed, part) draws one part's arguments, and reference() takes and returns one part's arrays. A program takes and returns all parts, laid end to end along the dimension named above; an argument that names none is the same for every part. Nothing has to cross between parts.
Inputs may be any that keep to these rules, and one draw needn't show every extreme that they name: `turn_persona_ids`: the 48 turns of each bank index use personas whose rows lie on exactly 4 bank indices (row // 32), 12 turns for each of them, naming exactly 2 distinct personas of each. A permutation of the window's personas; row persona_bank_row[w] of adapter_down_factor and adapter_up_factor is persona w's adapter.
All inputs are finite; a program needn't handle non-finite values.
Results may differ from the reference program's by a relative error of at most 0.014.
Values may be sent and summed in bfloat16 or wider, within the bound.
A program may use at most 128 MiB of HBM per device.

```python
import jax
import jax.numpy as jnp
from jax import lax

MODEL_WIDTH = 8192
KEY_VALUE_WIDTH = 1024
ADAPTER_RANK = 64
SEG = 16
OWNERS_DEV = 4
CAP = 12
SLOTS = 32
TURN_DEV = 48
TOKENS = 3072
WINDOW_PERSONAS = 128
N_BANK = 4
N_TENSOR = 4


def slot_table(key):
    return jax.random.permutation(jax.random.fold_in(key, 5), WINDOW_PERSONAS).astype(jnp.int32)


def draw_persona_bank_row(key, part):
    table = slot_table(key)
    return table


def draw_turn_persona_ids(key, part):
    table = slot_table(key)
    key = jax.random.fold_in(key, 7)
    keys = jax.random.split(key, 7)
    hottest = jax.random.randint(keys[0], (), 0, N_BANK)
    owner_ids = jnp.arange(N_BANK, dtype=jnp.int32)
    popular = jax.random.randint(keys[1], (N_BANK,), 0, 4)
    noise = jax.random.randint(keys[2], (N_BANK, N_BANK), 0, 1 << 14)
    score = popular[None, :] * (1 << 24) + noise * N_BANK + owner_ids[None, :]
    score = score + (owner_ids[None, :] == hottest).astype(jnp.int32) * (1 << 28)
    chosen = lax.top_k(score, OWNERS_DEV)[1].astype(jnp.int32)
    first = jax.random.randint(keys[3], (N_BANK, OWNERS_DEV), 0, SLOTS)
    offset = jax.random.randint(keys[4], (N_BANK, OWNERS_DEV), 1, SLOTS)
    second = (first + offset) % SLOTS
    split_at = jax.random.randint(keys[5], (N_BANK, OWNERS_DEV), 1, CAP)
    position = jnp.arange(CAP, dtype=jnp.int32)
    local = jnp.where(position[None, None, :] < split_at[:, :, None], first[:, :, None], second[:, :, None])
    global_slot = chosen[:, :, None] * SLOTS + local
    inverse = jnp.argsort(table, stable=True).astype(jnp.int32)
    persona = inverse[global_slot].reshape(N_BANK, TURN_DEV)
    ranking = jax.random.randint(keys[6], (N_BANK, TURN_DEV), 0, 1 << 20) * TURN_DEV + jnp.arange(TURN_DEV, dtype=jnp.int32)[None, :]
    order = jnp.argsort(ranking, axis=1, stable=True)
    persona = jnp.take_along_axis(persona, order, axis=1)
    return persona.reshape(-1).astype(jnp.int32)


def shard_levels(own_key, dims, pieces, low, largest):
    factor_of = 1.0
    for axis_at, parts in pieces:
        heights = jax.random.uniform(jax.random.fold_in(jax.random.fold_in(own_key, 6), axis_at), (parts,), jnp.float32, low / len(pieces), largest / len(pieces))
        factor_of = factor_of * jnp.repeat(jnp.exp(heights), dims[axis_at] // parts).reshape((-1,) + (1,) * (len(dims) - 1 - axis_at))
    return factor_of


def centred(stream_key, dims, scale, most, cuts=(), kind=jnp.bfloat16):
    entries = scale * jax.random.normal(stream_key, dims, jnp.float32)
    if cuts:
        entries = entries * shard_levels(stream_key, dims, cuts, -0.22, 0.18)
    return jnp.clip(entries, -most, most).astype(kind)


def setup_inputs(seed: int = 0, part: int = 0) -> dict:
    key_list = jax.random.split(jax.random.key(seed), 8)
    part_keys = jax.random.split(jax.random.fold_in(key_list[7], part), 8)
    normed = centred(part_keys[0], (TOKENS, MODEL_WIDTH), 1.0, 6.0, ((0, 4), (1, 4)))
    turn_persona_ids = draw_turn_persona_ids(jax.random.fold_in(jax.random.fold_in(key_list[7], part), 71), part)
    persona_bank_row = draw_persona_bank_row(jax.random.fold_in(jax.random.fold_in(key_list[7], part), 71), part)
    key_weight = centred(key_list[3], (MODEL_WIDTH, KEY_VALUE_WIDTH), MODEL_WIDTH ** -0.5, 0.0625, ((0, 4),))
    value_weight = centred(key_list[4], (MODEL_WIDTH, KEY_VALUE_WIDTH), MODEL_WIDTH ** -0.5, 0.0625, ((0, 4),))
    adapter_down_factor = centred(part_keys[5], (WINDOW_PERSONAS, ADAPTER_RANK, MODEL_WIDTH), MODEL_WIDTH ** -0.5, 0.0625, ((0, 4), (2, 4)))
    adapter_up_factor = centred(part_keys[6], (WINDOW_PERSONAS, ADAPTER_RANK, KEY_VALUE_WIDTH), (4 * ADAPTER_RANK) ** -0.5, 0.375, ((0, 4), (2, 4)))
    return {"normed": normed, "turn_persona_ids": turn_persona_ids, "persona_bank_row": persona_bank_row, "key_weight": key_weight, "value_weight": value_weight, "adapter_down_factor": adapter_down_factor, "adapter_up_factor": adapter_up_factor}


adapter_scale = 2.0


def reference(normed, turn_persona_ids, persona_bank_row, key_weight, value_weight, adapter_down_factor, adapter_up_factor):
    every_token = normed.shape[0]
    width = normed.shape[1]
    block = width // N_TENSOR

    def add_block(index, total):
        start = (index * block)
        feats = lax.dynamic_slice_in_dim(normed, start, block, 1)
        key_rows = lax.dynamic_slice_in_dim(key_weight, start, block, 0)
        value_rows = lax.dynamic_slice_in_dim(value_weight, start, block, 0)
        partial_both = jnp.stack([jnp.dot(feats, key_rows, preferred_element_type=jnp.float32),
                                  jnp.dot(feats, value_rows, preferred_element_type=jnp.float32)])
        rounded = lax.optimization_barrier(partial_both.astype(jnp.bfloat16))
        return total + rounded.astype(jnp.float32)

    partial_sums = lax.fori_loop(0, N_TENSOR, add_block, jnp.zeros((2, every_token, KEY_VALUE_WIDTH), jnp.float32))

    turns_all = turn_persona_ids.shape[0]
    slot_all = persona_bank_row[turn_persona_ids]
    rows_per_turn = normed.reshape(N_BANK, turns_all // N_BANK, SEG, width)
    bank_slot_blocks = slot_all.reshape(N_BANK, turns_all // N_BANK)

    def adapter_block(element_entry):
        row_portion, slot_portion = element_entry
        lowered_input = adapter_down_factor[slot_portion].astype(jnp.float32)
        inner = jnp.einsum('tsd,trd->tsr', row_portion.astype(jnp.float32), lowered_input)
        inner_reduced = lax.optimization_barrier(inner.astype(jnp.bfloat16)).astype(jnp.float32)
        raised_output = adapter_up_factor[slot_portion].astype(jnp.float32)
        return jnp.einsum('tsr,trk->tsk', inner_reduced, raised_output)

    value_update = lax.map(adapter_block, (rows_per_turn, bank_slot_blocks)).reshape(every_token, KEY_VALUE_WIDTH)
    keys = partial_sums[0].astype(jnp.bfloat16)
    values = (partial_sums[1] + adapter_scale * value_update).astype(jnp.bfloat16)
    return keys, values
```

```python
import functools

import jax
import jax.numpy as jnp
from jax import lax
from jax.experimental import pallas as pl
from jax.experimental.pallas import tpu as pltpu
from jax.sharding import PartitionSpec as P

ADAPTER_SCALE = 2.0
LANES = 128
BF16 = jnp.bfloat16
F32 = jnp.float32


def kernel(
    n_t,
    n_b,
    step,
    ids,
    table,
    normed_h,
    kw_h,
    vw_h,
    down_h,
    up_h,
    keys_o,
    vals_o,
    x,
    w,
    down,
    up,
    part,
    rcv,
    gbuf,
    gs,
    pts,
    asend,
    arecv,
    big,
    dup,
    own,
    rin,
    sin,
    e,
    delta,
    acc,
    xsem,
    wsem,
    dsem,
    gsem,
    ids_s,
    ids_r,
    ad_s,
    ad_r,
    ssem,
    rsem,
    in_s,
    in_r,
):
    i = lax.axis_index("tensor")
    me = lax.axis_index("bank")
    tokens, feats = x.shape
    slots, rank, _ = down.shape
    cols = up.shape[2]
    turns = ids.shape[0]
    seg = tokens // turns
    chunks = tokens // step
    pair = 2 * rank
    half = tokens // 2
    blocks = n_b * pair // LANES

    def rows_of(c):
        return pl.ds(pl.multiple_of(c * step, step), step)

    def w_copies(d):
        at = pl.ds(pl.multiple_of(d * cols, cols), cols)
        return (
            pltpu.make_async_copy(kw_h.at[:, at], w.at[d, :, pl.ds(0, cols)], wsem.at[d, 0]),
            pltpu.make_async_copy(vw_h.at[:, at], w.at[d, :, pl.ds(cols, cols)], wsem.at[d, 1]),
        )

    def x_copy(c):
        return pltpu.make_async_copy(normed_h.at[rows_of(c)], x.at[rows_of(c)], xsem.at[c])

    down_copy = pltpu.make_async_copy(down_h, down, dsem.at[0])
    up_copy = pltpu.make_async_copy(up_h, up, dsem.at[1])

    def dest(s):
        k = n_t - 1 - s // 2
        return i + k * (1 - 2 * lax.rem(s, 2))

    def load_w(s, _):
        d = dest(s)

        @pl.when((d >= 0) & (d < n_t))
        def _():
            for copy in w_copies(d):
                copy.start()

        return 0

    x_copy(0).start()
    lax.fori_loop(0, 2, load_w, 0)
    for c in range(1, chunks):
        x_copy(c).start()
    down_copy.start()
    up_copy.start()
    lax.fori_loop(2, 2 * n_t - 1, load_w, 0)

    barrier = pltpu.get_barrier_semaphore()

    def greet(k, _):
        pl.semaphore_signal(barrier, inc=1, device_id={"bank": lax.rem(me + k, n_b)})
        return 0

    lax.fori_loop(1, n_b, greet, 0)

    @pl.when(i > 0)
    def _():
        pl.semaphore_signal(barrier, inc=1, device_id={"tensor": i - 1})

    @pl.when(i < n_t - 1)
    def _():
        pl.semaphore_signal(barrier, inc=1, device_id={"tensor": i + 1})

    lane8 = lax.broadcasted_iota(jnp.int32, (8, LANES), 1)
    row8 = lax.broadcasted_iota(jnp.int32, (8, LANES), 0)

    def scan_turn(t, carry):
        low, high = carry
        slot = table[ids[t]]
        owner = slot // slots
        local = slot - owner * slots
        pts[t] = slot
        here = lane8 == owner
        low = jnp.where(here, jnp.minimum(low, local), low)
        high = jnp.where(here, jnp.maximum(high, local), high)
        return low, high

    low, high = lax.fori_loop(
        0,
        turns,
        scan_turn,
        (jnp.full((8, LANES), slots - 1, jnp.int32), jnp.zeros((8, LANES), jnp.int32)),
    )
    gbuf[me] = jnp.where(row8 == 0, low, high)

    neighbours = (n_b - 1) + (i > 0).astype(jnp.int32) + (i < n_t - 1).astype(jnp.int32)
    pl.semaphore_wait(barrier, neighbours)

    def ids_msg(d, slot):
        return pltpu.make_async_remote_copy(
            src_ref=gbuf.at[me],
            dst_ref=gbuf.at[slot],
            send_sem=ids_s.at[d],
            recv_sem=ids_r.at[slot],
            device_id={"bank": d},
        )

    def send_ids(k, _):
        ids_msg(lax.rem(me + k, n_b), me).start()
        return 0

    lax.fori_loop(1, n_b, send_ids, 0)

    def msg(d, c):
        left = (d < i).astype(jnp.int32)
        return pltpu.make_async_remote_copy(
            src_ref=part.at[d, rows_of(c)],
            dst_ref=rcv.at[left, d, rows_of(c)],
            send_sem=ssem.at[d, c],
            recv_sem=rsem.at[left, d, c],
            device_id={"tensor": i + 1 - 2 * left},
        )

    def arrival(left, d, c):
        return pltpu.make_async_remote_copy(
            src_ref=part.at[d, rows_of(c)],
            dst_ref=rcv.at[left, d, rows_of(c)],
            send_sem=ssem.at[d, c],
            recv_sem=rsem.at[left, d, c],
            device_id={"tensor": (i + 1) - 2 * (i > 0).astype(jnp.int32)},
        )

    at_end = (i == 0) | (i == n_t - 1)

    def project(s, _):
        d = dest(s)

        @pl.when((d >= 0) & (d < n_t))
        def _():
            for copy in w_copies(d):
                copy.wait()

            def chunk(c, _):
                @pl.when(waits_x(s))
                def _():
                    x_copy(c).wait()

                part[d, rows_of(c)] = jnp.dot(
                    x[rows_of(c), :], w[d], preferred_element_type=F32
                ).astype(BF16)

                @pl.when(at_end & (s < 2 * n_t - 4))
                def _():
                    msg(d, c).start()

                return 0

            lax.fori_loop(0, chunks, chunk, 0)

        return 0

    first = 2 * (n_t - 1 - jnp.maximum(i, n_t - 1 - i)) + (i > n_t - 1 - i).astype(jnp.int32)

    def waits_x(s):
        return s == first

    lax.fori_loop(0, 2, project, 0)

    def ids_in(k, _):
        ids_msg(lax.rem(me + k, n_b), lax.rem(me + k, n_b)).wait_recv()
        return 0

    lax.fori_loop(1, n_b, ids_in, 0)
    to_smem = pltpu.make_async_copy(gbuf, gs, gsem.at[0])
    to_smem.start()
    to_smem.wait()
    down_copy.wait()
    up_copy.wait()

    def bank_rows(d):
        return pl.ds(pl.multiple_of(d * pair, pair), pair)

    def fill(d, to):
        for j in range(2):
            slot = gs[d, j, me]
            at = pl.ds(pl.multiple_of(d * pair + j * rank, rank), rank)
            to[at, pl.ds(0, feats)] = down[slot]
            to[at, pl.ds(feats, cols)] = up[slot]

    def adapter_msg(d, slot):
        return pltpu.make_async_remote_copy(
            src_ref=asend.at[bank_rows(d)],
            dst_ref=arecv.at[bank_rows(slot)],
            send_sem=ad_s.at[d],
            recv_sem=ad_r.at[slot],
            device_id={"bank": d},
        )

    def send_adapter(k, _):
        d = lax.rem(me + k, n_b)
        fill(d, asend)
        adapter_msg(d, me).start()
        return 0

    lax.fori_loop(1, n_b, send_adapter, 0)
    fill(me, arecv)

    lax.fori_loop(2, 2 * n_t - 1, project, 0)

    def relay(d, left):
        def chunk(c, _):
            arrival(left, d, c).wait_recv()
            part[d, rows_of(c)] = (
                part[d, rows_of(c)].astype(F32) + rcv[left, d, rows_of(c)].astype(F32)
            ).astype(BF16)
            msg(d, c).start()
            return 0

        return chunk

    def own_start(d):
        def chunk(c, _):
            msg(d, c).start()
            return 0

        return chunk

    def relays(j, _):
        def chunk(c, _):
            right = n_t - 1 - j

            @pl.when((right > i) & (i > 0))
            def _():
                relay(right, 0)(c, 0)

            @pl.when((j < i) & (i < n_t - 1))
            def _():
                relay(j, 1)(c, 0)

            return 0

        return lax.fori_loop(0, chunks, chunk, 0)

    @pl.when((i > 0) & (i < n_t - 1))
    def _():
        lax.fori_loop(0, n_t - 1, relays, 0)

    def adapters_in(k, _):
        d = lax.rem(me + k, n_b)
        adapter_msg(d, d).wait_recv()
        return 0

    lax.fori_loop(1, n_b, adapters_in, 0)
    lane = lax.broadcasted_iota(jnp.int32, (seg, LANES), 1)
    turn_lane = lane // rank

    def choose(t, _):
        slot = pts[t]
        owner = slot // slots
        local = slot - owner * slots
        pts[t] = owner * 2 + (local != gs[me, 0, owner]).astype(jnp.int32)
        return 0

    lax.fori_loop(0, turns, choose, 0)

    def rank_chunk(c, _):
        big[...] = lax.dot_general(
            x[rows_of(c), :],
            arecv[:, :feats],
            (((1,), (1,)), ((), ())),
            preferred_element_type=F32,
        )

        def pick(t, _):
            p = pts[c * (step // seg) + t]
            at = pl.ds(pl.multiple_of(t * seg, seg), seg)
            total = jnp.zeros((seg, LANES), F32)
            for b in range(blocks):
                total = total + jnp.where(
                    turn_lane + 2 * b == p, big[at, b * LANES : (b + 1) * LANES], 0.0
                )
            total = total + pltpu.roll(total, rank, 1)
            dup[pl.ds(pl.multiple_of(c * step + t * seg, seg), seg), :] = total
            return 0

        return lax.fori_loop(0, step // seg, pick, 0)

    lax.fori_loop(0, chunks, rank_chunk, 0)
    low_lane = lax.broadcasted_iota(jnp.int32, (half, LANES), 1) < rank
    own[...] = jnp.where(low_lane, dup[pl.ds(0, half), :], dup[pl.ds(half, half), :])

    def inner_msg(left):
        return pltpu.make_async_remote_copy(
            src_ref=sin.at[left],
            dst_ref=rin.at[left],
            send_sem=in_s.at[left],
            recv_sem=in_r.at[left],
            device_id={"tensor": i + 1 - 2 * left},
        )

    def inner_in(left):
        return pltpu.make_async_remote_copy(
            src_ref=sin.at[left],
            dst_ref=rin.at[left],
            send_sem=in_s.at[left],
            recv_sem=in_r.at[left],
            device_id={"tensor": (i + 1) - 2 * (i > 0).astype(jnp.int32)},
        )

    @pl.when(i == 0)
    def _():
        sin[0] = own[...].astype(BF16)
        inner_msg(0).start()

    @pl.when(i == n_t - 1)
    def _():
        sin[1] = own[...].astype(BF16)
        inner_msg(1).start()

    @pl.when(i == 0)
    def _():
        lax.fori_loop(0, chunks, own_start(1), 0)

    @pl.when(i == n_t - 1)
    def _():
        lax.fori_loop(0, chunks, own_start(n_t - 2), 0)

    dup[pl.ds(0, half), :] = own[...]

    @pl.when(i > 0)
    def _():
        inner_in(0).wait_recv()
        before = rin[0].astype(F32)
        dup[pl.ds(0, half), :] += before

        @pl.when(i < n_t - 1)
        def _():
            sin[0] = (own[...] + before).astype(BF16)
            inner_msg(0).start()

    @pl.when(i < n_t - 1)
    def _():
        inner_in(1).wait_recv()
        after = rin[1].astype(F32)
        dup[pl.ds(0, half), :] += after

        @pl.when(i > 0)
        def _():
            sin[1] = (own[...] + after).astype(BF16)
            inner_msg(1).start()

    total = dup[pl.ds(0, half), :].astype(BF16).astype(F32)
    turned = pltpu.roll(total, rank, 1)
    dup[pl.ds(0, half), :] = jnp.where(low_lane, total, turned)
    dup[pl.ds(half, half), :] = jnp.where(low_lane, turned, total)

    def spread(t, _):
        p = pts[t]
        at = pl.ds(pl.multiple_of(t * seg, seg), seg)
        mine = dup[at, :]
        for b in range(blocks):
            e[at, b * LANES : (b + 1) * LANES] = jnp.where(turn_lane + 2 * b == p, mine, 0.0).astype(
                BF16
            )
        return 0

    lax.fori_loop(0, turns, spread, 0)

    def raise_chunk(c, _):
        delta[rows_of(c), :] = jnp.dot(
            e[rows_of(c), :], arecv[:, feats:], preferred_element_type=F32
        )
        return 0

    lax.fori_loop(0, chunks, raise_chunk, 0)

    def finish(c, _):
        acc[...] = part[i, rows_of(c)].astype(F32)

        @pl.when(i > 0)
        def _():
            arrival(0, i, c).wait_recv()
            acc[...] += rcv[0, i, rows_of(c)].astype(F32)

        @pl.when(i < n_t - 1)
        def _():
            arrival(1, i, c).wait_recv()
            acc[...] += rcv[1, i, rows_of(c)].astype(F32)

        keys_o[rows_of(c), :] = acc[:, :cols].astype(BF16)
        vals_o[rows_of(c), :] = (acc[:, cols:] + ADAPTER_SCALE * delta[rows_of(c), :]).astype(BF16)
        return 0

    lax.fori_loop(0, chunks, finish, 0)

    def sent(d, _):
        @pl.when(d != i)
        def _():
            def chunk(c, _):
                msg(d, c).wait_send()
                return 0

            lax.fori_loop(0, chunks, chunk, 0)

        return 0

    lax.fori_loop(0, n_t, sent, 0)

    def bank_sent(k, _):
        d = lax.rem(me + k, n_b)
        ids_msg(d, me).wait_send()
        adapter_msg(d, me).wait_send()
        return 0

    lax.fori_loop(1, n_b, bank_sent, 0)

    @pl.when(i < n_t - 1)
    def _():
        inner_msg(0).wait_send()

    @pl.when(i > 0)
    def _():
        inner_msg(1).wait_send()


def shards(
    n_t,
    n_b,
    normed,
    turn_persona_ids,
    persona_bank_row,
    key_weight,
    value_weight,
    adapter_down_factor,
    adapter_up_factor,
):
    tokens, feats = normed.shape
    slots, rank, cols = adapter_up_factor.shape
    turns = turn_persona_ids.shape[0]
    step = 256
    chunks = tokens // step
    dma = pltpu.SemaphoreType.DMA
    any_space = pl.BlockSpec(memory_space=pl.ANY)
    smem = pl.BlockSpec(memory_space=pltpu.SMEM)
    vmem = pl.BlockSpec(memory_space=pltpu.VMEM)
    out = jax.ShapeDtypeStruct((tokens, cols), BF16)
    return pl.pallas_call(
        functools.partial(kernel, n_t, n_b, step),
        out_shape=(out, out),
        in_specs=[smem, smem] + [any_space] * 5,
        out_specs=(vmem, vmem),
        scratch_shapes=[
            pltpu.VMEM((tokens, feats), BF16),
            pltpu.VMEM((n_t, feats, 2 * cols), BF16),
            pltpu.VMEM((slots, rank, feats), BF16),
            pltpu.VMEM((slots, rank, cols), BF16),
            pltpu.VMEM((n_t, tokens, 2 * cols), BF16),
            pltpu.VMEM((2, n_t, tokens, 2 * cols), BF16),
            pltpu.VMEM((n_b, 8, LANES), jnp.int32),
            pltpu.SMEM((n_b, 8, LANES), jnp.int32),
            pltpu.SMEM((turns,), jnp.int32),
            pltpu.VMEM((n_b * 2 * rank, feats + cols), BF16),
            pltpu.VMEM((n_b * 2 * rank, feats + cols), BF16),
            pltpu.VMEM((step, n_b * 2 * rank), F32),
            pltpu.VMEM((tokens, LANES), F32),
            pltpu.VMEM((tokens // 2, LANES), F32),
            pltpu.VMEM((2, tokens // 2, LANES), BF16),
            pltpu.VMEM((2, tokens // 2, LANES), BF16),
            pltpu.VMEM((tokens, n_b * 2 * rank), BF16),
            pltpu.VMEM((tokens, cols), F32),
            pltpu.VMEM((step, 2 * cols), F32),
            dma((chunks,)),
            dma((n_t, 2)),
            dma((2,)),
            dma((1,)),
            dma((n_b,)),
            dma((n_b,)),
            dma((n_b,)),
            dma((n_b,)),
            dma((n_t, chunks)),
            dma((2, n_t, chunks)),
            dma((2,)),
            dma((2,)),
        ],
        compiler_params=pltpu.CompilerParams(
            collective_id=0, has_side_effects=True, vmem_limit_bytes=58 * 1024 * 1024
        ),
        cost_estimate=pl.CostEstimate(
            flops=4 * tokens * feats * cols * n_t,
            bytes_accessed=2 * (tokens * feats + 2 * feats * cols * n_t + slots * rank * feats),
            transcendentals=0,
        ),
    )(
        turn_persona_ids,
        persona_bank_row,
        normed,
        key_weight,
        value_weight,
        adapter_down_factor,
        adapter_up_factor,
    )


def solution(mesh):
    placed = (
        P(("groups", "bank"), "tensor"),
        P(("groups", "bank")),
        P("groups"),
        P("tensor", None),
        P("tensor", None),
        P(("groups", "bank"), None, "tensor"),
        P(("groups", "bank"), None, "tensor"),
    )
    return jax.shard_map(
        functools.partial(shards, mesh.shape["tensor"], mesh.shape["bank"]),
        mesh=mesh,
        in_specs=placed,
        out_specs=(P(("groups", "bank"), "tensor"), P(("groups", "bank"), "tensor")),
        check_vma=False,
    )
```

```python
import functools

import jax
import jax.numpy as jnp
from jax import lax
from jax.experimental import pallas as pl
from jax.experimental.pallas import tpu as pltpu
from jax.sharding import PartitionSpec as P

ADAPTER_SCALE = 2.0
LANES = 128
BF16 = jnp.bfloat16
F32 = jnp.float32


def kernel(
    n_t,
    n_b,
    step,
    ids,
    table,
    normed_h,
    kw_h,
    vw_h,
    down_h,
    up_h,
    keys_o,
    vals_o,
    x,
    w,
    down,
    up,
    part,
    rcv,
    gbuf,
    gs,
    pts,
    asend,
    arecv,
    big,
    dup,
    own,
    rin,
    sin,
    e,
    delta,
    acc,
    xsem,
    wsem,
    dsem,
    gsem,
    ids_s,
    ids_r,
    ad_s,
    ad_r,
    ssem,
    rsem,
    in_s,
    in_r,
):
    i = lax.axis_index("tensor")
    me = lax.axis_index("bank")
    tokens, feats = x.shape
    slots, rank, _ = down.shape
    cols = up.shape[2]
    turns = ids.shape[0]
    seg = tokens // turns
    chunks = tokens // step
    pair = 2 * rank
    half = tokens // 2
    blocks = n_b * pair // LANES

    def rows_of(c):
        return pl.ds(pl.multiple_of(c * step, step), step)

    def w_copies(d):
        at = pl.ds(pl.multiple_of(d * cols, cols), cols)
        return (
            pltpu.make_async_copy(kw_h.at[:, at], w.at[d, :, pl.ds(0, cols)], wsem.at[d, 0]),
            pltpu.make_async_copy(vw_h.at[:, at], w.at[d, :, pl.ds(cols, cols)], wsem.at[d, 1]),
        )

    def x_copy(c):
        return pltpu.make_async_copy(normed_h.at[rows_of(c)], x.at[rows_of(c)], xsem.at[c])

    down_copy = pltpu.make_async_copy(down_h, down, dsem.at[0])
    up_copy = pltpu.make_async_copy(up_h, up, dsem.at[1])

    def dest(s):
        k = n_t - 1 - s // 2
        return i + k * (1 - 2 * lax.rem(s, 2))

    def load_w(s, _):
        d = dest(s)

        @pl.when((d >= 0) & (d < n_t))
        def _():
            for copy in w_copies(d):
                copy.start()

        return 0

    barrier = pltpu.get_barrier_semaphore()

    def greet(k, _):
        pl.semaphore_signal(barrier, inc=1, device_id={"bank": lax.rem(me + k, n_b)})
        return 0

    lax.fori_loop(1, n_b, greet, 0)

    @pl.when(i > 0)
    def _():
        pl.semaphore_signal(barrier, inc=1, device_id={"tensor": i - 1})

    @pl.when(i < n_t - 1)
    def _():
        pl.semaphore_signal(barrier, inc=1, device_id={"tensor": i + 1})

    first = 2 * (n_t - 1 - jnp.maximum(i, n_t - 1 - i)) + (i > n_t - 1 - i).astype(jnp.int32)
    x_copy(0).start()
    load_w(first, 0)
    for c in range(1, chunks):
        x_copy(c).start()

    lane8 = lax.broadcasted_iota(jnp.int32, (8, LANES), 1)
    row8 = lax.broadcasted_iota(jnp.int32, (8, LANES), 0)

    def scan_turn(t, carry):
        low, high = carry
        slot = table[ids[t]]
        owner = slot // slots
        local = slot - owner * slots
        pts[t] = slot
        here = lane8 == owner
        low = jnp.where(here, jnp.minimum(low, local), low)
        high = jnp.where(here, jnp.maximum(high, local), high)
        return low, high

    low, high = lax.fori_loop(
        0,
        turns,
        scan_turn,
        (jnp.full((8, LANES), slots - 1, jnp.int32), jnp.zeros((8, LANES), jnp.int32)),
    )
    gbuf[me] = jnp.where(row8 == 0, low, high)

    neighbours = (n_b - 1) + (i > 0).astype(jnp.int32) + (i < n_t - 1).astype(jnp.int32)
    pl.semaphore_wait(barrier, neighbours)

    def ids_msg(d, slot):
        return pltpu.make_async_remote_copy(
            src_ref=gbuf.at[me],
            dst_ref=gbuf.at[slot],
            send_sem=ids_s.at[d],
            recv_sem=ids_r.at[slot],
            device_id={"bank": d},
        )

    def send_ids(k, _):
        ids_msg(lax.rem(me + k, n_b), me).start()
        return 0

    lax.fori_loop(1, n_b, send_ids, 0)
    down_copy.start()
    up_copy.start()
    lax.fori_loop(first + 1, 2 * n_t - 1, load_w, 0)

    def msg(d, c):
        left = (d < i).astype(jnp.int32)
        return pltpu.make_async_remote_copy(
            src_ref=part.at[d, rows_of(c)],
            dst_ref=rcv.at[left, d, rows_of(c)],
            send_sem=ssem.at[d, c],
            recv_sem=rsem.at[left, d, c],
            device_id={"tensor": i + 1 - 2 * left},
        )

    def arrival(left, d, c):
        return pltpu.make_async_remote_copy(
            src_ref=part.at[d, rows_of(c)],
            dst_ref=rcv.at[left, d, rows_of(c)],
            send_sem=ssem.at[d, c],
            recv_sem=rsem.at[left, d, c],
            device_id={"tensor": (i + 1) - 2 * (i > 0).astype(jnp.int32)},
        )

    at_end = (i == 0) | (i == n_t - 1)

    def project(s, _):
        d = dest(s)

        @pl.when((d >= 0) & (d < n_t))
        def _():
            for copy in w_copies(d):
                copy.wait()

            def chunk(c, _):
                @pl.when(waits_x(s))
                def _():
                    x_copy(c).wait()

                part[d, rows_of(c)] = jnp.dot(
                    x[rows_of(c), :], w[d], preferred_element_type=F32
                ).astype(BF16)

                @pl.when(at_end & (s < 2 * n_t - 4))
                def _():
                    msg(d, c).start()

                return 0

            lax.fori_loop(0, chunks, chunk, 0)

        return 0

    def waits_x(s):
        return s == first

    lax.fori_loop(0, 2, project, 0)

    def ids_in(k, _):
        ids_msg(lax.rem(me + k, n_b), lax.rem(me + k, n_b)).wait_recv()
        return 0

    lax.fori_loop(1, n_b, ids_in, 0)
    to_smem = pltpu.make_async_copy(gbuf, gs, gsem.at[0])
    to_smem.start()
    to_smem.wait()
    down_copy.wait()
    up_copy.wait()

    def bank_rows(d):
        return pl.ds(pl.multiple_of(d * pair, pair), pair)

    def fill(d, to):
        for j in range(2):
            slot = gs[d, j, me]
            at = pl.ds(pl.multiple_of(d * pair + j * rank, rank), rank)
            to[at, pl.ds(0, feats)] = down[slot]
            to[at, pl.ds(feats, cols)] = up[slot]

    def adapter_msg(d, slot):
        return pltpu.make_async_remote_copy(
            src_ref=asend.at[bank_rows(d)],
            dst_ref=arecv.at[bank_rows(slot)],
            send_sem=ad_s.at[d],
            recv_sem=ad_r.at[slot],
            device_id={"bank": d},
        )

    def send_adapter(k, _):
        d = lax.rem(me + k, n_b)
        fill(d, asend)
        adapter_msg(d, me).start()
        return 0

    lax.fori_loop(1, n_b, send_adapter, 0)
    fill(me, arecv)

    lax.fori_loop(2, 2 * n_t - 1, project, 0)

    near = (2 * i > n_t - 1).astype(jnp.int32)
    inside = ((i > 0) & (i < n_t - 1)).astype(jnp.int32)
    near_total = inside * chunks * jnp.maximum(i, n_t - 1 - i)
    far_total = inside * chunks * jnp.minimum(i, n_t - 1 - i)

    def relay(left, u):
        b = u // chunks
        c = u - b * chunks
        d = left * b + (1 - left) * (n_t - 1 - b)
        arrival(left, d, c).wait_recv()
        part[d, rows_of(c)] = (
            part[d, rows_of(c)].astype(F32) + rcv[left, d, rows_of(c)].astype(F32)
        ).astype(BF16)
        msg(d, c).start()

    def relays(u, _):
        @pl.when(u < near_total)
        def _():
            relay(near, u)

        @pl.when((u >= 1) & (u <= far_total))
        def _():
            relay(1 - near, u - 1)

        return 0

    def own_start(d):
        def chunk(c, _):
            msg(d, c).start()
            return 0

        return chunk

    split = jnp.maximum(near_total - 1, 0)
    lax.fori_loop(0, split, relays, 0)

    def adapters_in(k, _):
        d = lax.rem(me + k, n_b)
        adapter_msg(d, d).wait_recv()
        return 0

    lax.fori_loop(1, n_b, adapters_in, 0)
    lane = lax.broadcasted_iota(jnp.int32, (seg, LANES), 1)
    turn_lane = lane // rank

    def choose(t, _):
        slot = pts[t]
        owner = slot // slots
        local = slot - owner * slots
        pts[t] = owner * 2 + (local != gs[me, 0, owner]).astype(jnp.int32)
        return 0

    lax.fori_loop(0, turns, choose, 0)

    def rank_chunk(c, _):
        big[...] = lax.dot_general(
            x[rows_of(c), :],
            arecv[:, :feats],
            (((1,), (1,)), ((), ())),
            preferred_element_type=F32,
        )

        def pick(t, _):
            p = pts[c * (step // seg) + t]
            at = pl.ds(pl.multiple_of(t * seg, seg), seg)
            total = jnp.zeros((seg, LANES), F32)
            for b in range(blocks):
                total = total + jnp.where(
                    turn_lane + 2 * b == p, big[at, b * LANES : (b + 1) * LANES], 0.0
                )
            total = total + pltpu.roll(total, rank, 1)
            dup[pl.ds(pl.multiple_of(c * step + t * seg, seg), seg), :] = total
            return 0

        return lax.fori_loop(0, step // seg, pick, 0)

    lax.fori_loop(0, chunks, rank_chunk, 0)
    low_lane = lax.broadcasted_iota(jnp.int32, (half, LANES), 1) < rank
    own[...] = jnp.where(low_lane, dup[pl.ds(0, half), :], dup[pl.ds(half, half), :])

    def inner_msg(left):
        return pltpu.make_async_remote_copy(
            src_ref=sin.at[left],
            dst_ref=rin.at[left],
            send_sem=in_s.at[left],
            recv_sem=in_r.at[left],
            device_id={"tensor": i + 1 - 2 * left},
        )

    def inner_in(left):
        return pltpu.make_async_remote_copy(
            src_ref=sin.at[left],
            dst_ref=rin.at[left],
            send_sem=in_s.at[left],
            recv_sem=in_r.at[left],
            device_id={"tensor": (i + 1) - 2 * (i > 0).astype(jnp.int32)},
        )

    @pl.when(i == 0)
    def _():
        sin[0] = own[...].astype(BF16)
        inner_msg(0).start()

    @pl.when(i == n_t - 1)
    def _():
        sin[1] = own[...].astype(BF16)
        inner_msg(1).start()

    @pl.when(i == 0)
    def _():
        lax.fori_loop(0, chunks, own_start(1), 0)

    @pl.when(i == n_t - 1)
    def _():
        lax.fori_loop(0, chunks, own_start(n_t - 2), 0)

    lax.fori_loop(split, near_total + 1, relays, 0)
    dup[pl.ds(0, half), :] = own[...]

    def exchange(k, _):
        left = near + k - 2 * near * k

        @pl.when(((left == 0) & (i > 0)) | ((left == 1) & (i < n_t - 1)))
        def _():
            inner_in(left).wait_recv()
            came = rin[left].astype(F32)
            dup[pl.ds(0, half), :] += came

            @pl.when(inside == 1)
            def _():
                sin[left] = (own[...] + came).astype(BF16)
                inner_msg(left).start()

        return 0

    lax.fori_loop(0, 2, exchange, 0)
    total = dup[pl.ds(0, half), :].astype(BF16).astype(F32)
    turned = pltpu.roll(total, rank, 1)
    dup[pl.ds(0, half), :] = jnp.where(low_lane, total, turned)
    dup[pl.ds(half, half), :] = jnp.where(low_lane, turned, total)

    def spread(t, _):
        p = pts[t]
        at = pl.ds(pl.multiple_of(t * seg, seg), seg)
        mine = dup[at, :]
        for b in range(blocks):
            e[at, b * LANES : (b + 1) * LANES] = jnp.where(turn_lane + 2 * b == p, mine, 0.0).astype(
                BF16
            )
        return 0

    lax.fori_loop(0, turns, spread, 0)

    def raise_chunk(c, _):
        delta[rows_of(c), :] = jnp.dot(
            e[rows_of(c), :], arecv[:, feats:], preferred_element_type=F32
        )
        return 0

    lax.fori_loop(0, chunks, raise_chunk, 0)

    def finish(c, _):
        acc[...] = part[i, rows_of(c)].astype(F32)

        @pl.when(i > 0)
        def _():
            arrival(0, i, c).wait_recv()
            acc[...] += rcv[0, i, rows_of(c)].astype(F32)

        @pl.when(i < n_t - 1)
        def _():
            arrival(1, i, c).wait_recv()
            acc[...] += rcv[1, i, rows_of(c)].astype(F32)

        keys_o[rows_of(c), :] = acc[:, :cols].astype(BF16)
        vals_o[rows_of(c), :] = (acc[:, cols:] + ADAPTER_SCALE * delta[rows_of(c), :]).astype(BF16)
        return 0

    lax.fori_loop(0, chunks, finish, 0)

    def sent(d, _):
        @pl.when(d != i)
        def _():
            def chunk(c, _):
                msg(d, c).wait_send()
                return 0

            lax.fori_loop(0, chunks, chunk, 0)

        return 0

    lax.fori_loop(0, n_t, sent, 0)

    def bank_sent(k, _):
        d = lax.rem(me + k, n_b)
        ids_msg(d, me).wait_send()
        adapter_msg(d, me).wait_send()
        return 0

    lax.fori_loop(1, n_b, bank_sent, 0)

    @pl.when(i < n_t - 1)
    def _():
        inner_msg(0).wait_send()

    @pl.when(i > 0)
    def _():
        inner_msg(1).wait_send()


def shards(
    n_t,
    n_b,
    normed,
    turn_persona_ids,
    persona_bank_row,
    key_weight,
    value_weight,
    adapter_down_factor,
    adapter_up_factor,
):
    tokens, feats = normed.shape
    slots, rank, cols = adapter_up_factor.shape
    turns = turn_persona_ids.shape[0]
    step = 256
    chunks = tokens // step
    dma = pltpu.SemaphoreType.DMA
    any_space = pl.BlockSpec(memory_space=pl.ANY)
    smem = pl.BlockSpec(memory_space=pltpu.SMEM)
    vmem = pl.BlockSpec(memory_space=pltpu.VMEM)
    out = jax.ShapeDtypeStruct((tokens, cols), BF16)
    return pl.pallas_call(
        functools.partial(kernel, n_t, n_b, step),
        out_shape=(out, out),
        in_specs=[smem, smem] + [any_space] * 5,
        out_specs=(vmem, vmem),
        scratch_shapes=[
            pltpu.VMEM((tokens, feats), BF16),
            pltpu.VMEM((n_t, feats, 2 * cols), BF16),
            pltpu.VMEM((slots, rank, feats), BF16),
            pltpu.VMEM((slots, rank, cols), BF16),
            pltpu.VMEM((n_t, tokens, 2 * cols), BF16),
            pltpu.VMEM((2, n_t, tokens, 2 * cols), BF16),
            pltpu.VMEM((n_b, 8, LANES), jnp.int32),
            pltpu.SMEM((n_b, 8, LANES), jnp.int32),
            pltpu.SMEM((turns,), jnp.int32),
            pltpu.VMEM((n_b * 2 * rank, feats + cols), BF16),
            pltpu.VMEM((n_b * 2 * rank, feats + cols), BF16),
            pltpu.VMEM((step, n_b * 2 * rank), F32),
            pltpu.VMEM((tokens, LANES), F32),
            pltpu.VMEM((tokens // 2, LANES), F32),
            pltpu.VMEM((2, tokens // 2, LANES), BF16),
            pltpu.VMEM((2, tokens // 2, LANES), BF16),
            pltpu.VMEM((tokens, n_b * 2 * rank), BF16),
            pltpu.VMEM((tokens, cols), F32),
            pltpu.VMEM((step, 2 * cols), F32),
            dma((chunks,)),
            dma((n_t, 2)),
            dma((2,)),
            dma((1,)),
            dma((n_b,)),
            dma((n_b,)),
            dma((n_b,)),
            dma((n_b,)),
            dma((n_t, chunks)),
            dma((2, n_t, chunks)),
            dma((2,)),
            dma((2,)),
        ],
        compiler_params=pltpu.CompilerParams(
            collective_id=0, has_side_effects=True, vmem_limit_bytes=58 * 1024 * 1024
        ),
        cost_estimate=pl.CostEstimate(
            flops=4 * tokens * feats * cols * n_t,
            bytes_accessed=2 * (tokens * feats + 2 * feats * cols * n_t + slots * rank * feats),
            transcendentals=0,
        ),
    )(
        turn_persona_ids,
        persona_bank_row,
        normed,
        key_weight,
        value_weight,
        adapter_down_factor,
        adapter_up_factor,
    )


def solution(mesh):
    placed = (
        P(("groups", "bank"), "tensor"),
        P(("groups", "bank")),
        P("groups"),
        P("tensor", None),
        P("tensor", None),
        P(("groups", "bank"), None, "tensor"),
        P(("groups", "bank"), None, "tensor"),
    )
    return jax.shard_map(
        functools.partial(shards, mesh.shape["tensor"], mesh.shape["bank"]),
        mesh=mesh,
        in_specs=placed,
        out_specs=(P(("groups", "bank"), "tensor"), P(("groups", "bank"), "tensor")),
        check_vma=False,
    )
```

```python
import functools

import jax
import jax.numpy as jnp
from jax import lax
from jax.experimental import pallas as pl
from jax.experimental.pallas import tpu as pltpu
from jax.sharding import PartitionSpec as P

ADAPTER_SCALE = 2.0
LANES = 128
BF16 = jnp.bfloat16
F32 = jnp.float32


def kernel(
    n_t,
    n_b,
    step,
    ids,
    table,
    normed_h,
    kw_h,
    vw_h,
    down_h,
    up_h,
    keys_o,
    vals_o,
    x,
    w,
    down,
    up,
    part,
    rcv,
    gbuf,
    gs,
    pts,
    asend,
    arecv,
    big,
    dup,
    own,
    rin,
    sin,
    e,
    delta,
    acc,
    xsem,
    wsem,
    dsem,
    gsem,
    ids_s,
    ids_r,
    ad_s,
    ad_r,
    ssem,
    rsem,
    in_s,
    in_r,
):
    i = lax.axis_index("tensor")
    me = lax.axis_index("bank")
    tokens, feats = x.shape
    slots, rank, _ = down.shape
    cols = up.shape[2]
    turns = ids.shape[0]
    seg = tokens // turns
    chunks = tokens // step
    pair = 2 * rank
    half = tokens // 2
    blocks = n_b * pair // LANES

    def rows_of(c):
        return pl.ds(pl.multiple_of(c * step, step), step)

    def w_copies(d):
        at = pl.ds(pl.multiple_of(d * cols, cols), cols)
        return (
            pltpu.make_async_copy(kw_h.at[:, at], w.at[d, :, pl.ds(0, cols)], wsem.at[d, 0]),
            pltpu.make_async_copy(vw_h.at[:, at], w.at[d, :, pl.ds(cols, cols)], wsem.at[d, 1]),
        )

    def x_copy(c):
        return pltpu.make_async_copy(normed_h.at[rows_of(c)], x.at[rows_of(c)], xsem.at[c])

    down_copy = pltpu.make_async_copy(down_h, down, dsem.at[0])
    up_copy = pltpu.make_async_copy(up_h, up, dsem.at[1])

    def dest(s):
        k = n_t - 1 - s // 2
        return i + k * (1 - 2 * lax.rem(s, 2))

    def load_w(s, _):
        d = dest(s)

        @pl.when((d >= 0) & (d < n_t))
        def _():
            for copy in w_copies(d):
                copy.start()

        return 0

    barrier = pltpu.get_barrier_semaphore()

    def greet(k, _):
        pl.semaphore_signal(barrier, inc=1, device_id={"bank": lax.rem(me + k, n_b)})
        return 0

    lax.fori_loop(1, n_b, greet, 0)

    @pl.when(i > 0)
    def _():
        pl.semaphore_signal(barrier, inc=1, device_id={"tensor": i - 1})

    @pl.when(i < n_t - 1)
    def _():
        pl.semaphore_signal(barrier, inc=1, device_id={"tensor": i + 1})

    first = 2 * (n_t - 1 - jnp.maximum(i, n_t - 1 - i)) + (i > n_t - 1 - i).astype(jnp.int32)
    x_copy(0).start()
    load_w(first, 0)
    for c in range(1, chunks):
        x_copy(c).start()

    lane8 = lax.broadcasted_iota(jnp.int32, (8, LANES), 1)
    row8 = lax.broadcasted_iota(jnp.int32, (8, LANES), 0)

    def scan_turn(t, carry):
        low, high = carry
        slot = table[ids[t]]
        owner = slot // slots
        local = slot - owner * slots
        pts[t] = slot
        here = lane8 == owner
        low = jnp.where(here, jnp.minimum(low, local), low)
        high = jnp.where(here, jnp.maximum(high, local), high)
        return low, high

    low, high = lax.fori_loop(
        0,
        turns,
        scan_turn,
        (jnp.full((8, LANES), slots - 1, jnp.int32), jnp.zeros((8, LANES), jnp.int32)),
    )
    gbuf[me] = jnp.where(row8 == 0, low, high)

    neighbours = (n_b - 1) + (i > 0).astype(jnp.int32) + (i < n_t - 1).astype(jnp.int32)
    pl.semaphore_wait(barrier, neighbours)

    def ids_msg(d, slot):
        return pltpu.make_async_remote_copy(
            src_ref=gbuf.at[me],
            dst_ref=gbuf.at[slot],
            send_sem=ids_s.at[d],
            recv_sem=ids_r.at[slot],
            device_id={"bank": d},
        )

    def send_ids(k, _):
        ids_msg(lax.rem(me + k, n_b), me).start()
        return 0

    lax.fori_loop(1, n_b, send_ids, 0)
    down_copy.start()
    up_copy.start()
    lax.fori_loop(first + 1, 2 * n_t - 1, load_w, 0)

    def msg(d, c):
        left = (d < i).astype(jnp.int32)
        return pltpu.make_async_remote_copy(
            src_ref=part.at[d, rows_of(c)],
            dst_ref=rcv.at[left, d, rows_of(c)],
            send_sem=ssem.at[d, c],
            recv_sem=rsem.at[left, d, c],
            device_id={"tensor": i + 1 - 2 * left},
        )

    def arrival(left, d, c):
        return pltpu.make_async_remote_copy(
            src_ref=part.at[d, rows_of(c)],
            dst_ref=rcv.at[left, d, rows_of(c)],
            send_sem=ssem.at[d, c],
            recv_sem=rsem.at[left, d, c],
            device_id={"tensor": (i + 1) - 2 * (i > 0).astype(jnp.int32)},
        )

    at_end = (i == 0) | (i == n_t - 1)

    def project(s, _):
        d = dest(s)

        @pl.when((d >= 0) & (d < n_t))
        def _():
            for copy in w_copies(d):
                copy.wait()

            def chunk(c, _):
                @pl.when(waits_x(s))
                def _():
                    x_copy(c).wait()

                part[d, rows_of(c)] = jnp.dot(
                    x[rows_of(c), :], w[d], preferred_element_type=F32
                ).astype(BF16)

                @pl.when(at_end & (s < 2 * n_t - 4))
                def _():
                    msg(d, c).start()

                return 0

            lax.fori_loop(0, chunks, chunk, 0)

        return 0

    def waits_x(s):
        return s == first

    lax.fori_loop(0, 2, project, 0)

    def ids_in(k, _):
        ids_msg(lax.rem(me + k, n_b), lax.rem(me + k, n_b)).wait_recv()
        return 0

    lax.fori_loop(1, n_b, ids_in, 0)
    to_smem = pltpu.make_async_copy(gbuf, gs, gsem.at[0])
    to_smem.start()
    to_smem.wait()
    down_copy.wait()
    up_copy.wait()

    def bank_rows(d):
        return pl.ds(pl.multiple_of(d * pair, pair), pair)

    def fill(d, to):
        for j in range(2):
            slot = gs[d, j, me]
            at = pl.ds(pl.multiple_of(d * pair + j * rank, rank), rank)
            to[at, pl.ds(0, feats)] = down[slot]
            to[at, pl.ds(feats, cols)] = up[slot]

    def adapter_msg(d, slot):
        return pltpu.make_async_remote_copy(
            src_ref=asend.at[bank_rows(d)],
            dst_ref=arecv.at[bank_rows(slot)],
            send_sem=ad_s.at[d],
            recv_sem=ad_r.at[slot],
            device_id={"bank": d},
        )

    def send_adapter(k, _):
        d = lax.rem(me + k, n_b)
        fill(d, asend)
        adapter_msg(d, me).start()
        return 0

    lax.fori_loop(1, n_b, send_adapter, 0)
    fill(me, arecv)

    lax.fori_loop(2, 2 * n_t - 1, project, 0)

    near = (2 * i > n_t - 1).astype(jnp.int32)
    inside = ((i > 0) & (i < n_t - 1)).astype(jnp.int32)
    near_total = inside * chunks * jnp.maximum(i, n_t - 1 - i)
    far_total = inside * chunks * jnp.minimum(i, n_t - 1 - i)

    def relay(left, u):
        b = u // chunks
        c = u - b * chunks
        d = left * b + (1 - left) * (n_t - 1 - b)
        arrival(left, d, c).wait_recv()
        part[d, rows_of(c)] = (
            part[d, rows_of(c)].astype(F32) + rcv[left, d, rows_of(c)].astype(F32)
        ).astype(BF16)
        msg(d, c).start()

    def relays(u, _):
        @pl.when(u < near_total)
        def _():
            relay(near, u)

        @pl.when((u >= 1) & (u <= far_total))
        def _():
            relay(1 - near, u - 1)

        return 0

    def own_start(d):
        def chunk(c, _):
            msg(d, c).start()
            return 0

        return chunk

    split = jnp.maximum(near_total - 1, 0)
    lax.fori_loop(0, split, relays, 0)

    def adapters_in(k, _):
        d = lax.rem(me + k, n_b)
        adapter_msg(d, d).wait_recv()
        return 0

    lax.fori_loop(1, n_b, adapters_in, 0)
    lane = lax.broadcasted_iota(jnp.int32, (seg, LANES), 1)
    turn_lane = lane // rank

    def choose(t, _):
        slot = pts[t]
        owner = slot // slots
        local = slot - owner * slots
        pts[t] = owner * 2 + (local != gs[me, 0, owner]).astype(jnp.int32)
        return 0

    lax.fori_loop(0, turns, choose, 0)

    def rank_chunk(c, _):
        big[...] = lax.dot_general(
            x[rows_of(c), :],
            arecv[:, :feats],
            (((1,), (1,)), ((), ())),
            preferred_element_type=F32,
        )

        def pick(t, _):
            p = pts[c * (step // seg) + t]
            at = pl.ds(pl.multiple_of(t * seg, seg), seg)
            total = jnp.zeros((seg, LANES), F32)
            for b in range(blocks):
                total = total + jnp.where(
                    turn_lane + 2 * b == p, big[at, b * LANES : (b + 1) * LANES], 0.0
                )
            total = total + pltpu.roll(total, rank, 1)
            dup[pl.ds(pl.multiple_of(c * step + t * seg, seg), seg), :] = total
            return 0

        return lax.fori_loop(0, step // seg, pick, 0)

    lax.fori_loop(0, chunks, rank_chunk, 0)
    low_lane = lax.broadcasted_iota(jnp.int32, (half, LANES), 1) < rank
    own[...] = jnp.where(low_lane, dup[pl.ds(0, half), :], dup[pl.ds(half, half), :])

    def inner_msg(left):
        return pltpu.make_async_remote_copy(
            src_ref=sin.at[left],
            dst_ref=rin.at[left],
            send_sem=in_s.at[left],
            recv_sem=in_r.at[left],
            device_id={"tensor": i + 1 - 2 * left},
        )

    def inner_in(left):
        return pltpu.make_async_remote_copy(
            src_ref=sin.at[left],
            dst_ref=rin.at[left],
            send_sem=in_s.at[left],
            recv_sem=in_r.at[left],
            device_id={"tensor": (i + 1) - 2 * (i > 0).astype(jnp.int32)},
        )

    @pl.when(i == 0)
    def _():
        sin[0] = own[...].astype(BF16)
        inner_msg(0).start()

    @pl.when(i == n_t - 1)
    def _():
        sin[1] = own[...].astype(BF16)
        inner_msg(1).start()

    @pl.when(i == 0)
    def _():
        lax.fori_loop(0, chunks, own_start(1), 0)

    @pl.when(i == n_t - 1)
    def _():
        lax.fori_loop(0, chunks, own_start(n_t - 2), 0)

    lax.fori_loop(split, near_total + 1, relays, 0)
    dup[pl.ds(0, half), :] = own[...]

    def exchange(k, _):
        left = near + k - 2 * near * k

        @pl.when(((left == 0) & (i > 0)) | ((left == 1) & (i < n_t - 1)))
        def _():
            inner_in(left).wait_recv()
            came = rin[left].astype(F32)
            dup[pl.ds(0, half), :] += came

            @pl.when(inside == 1)
            def _():
                sin[left] = (own[...] + came).astype(BF16)
                inner_msg(left).start()

        return 0

    lax.fori_loop(0, 2, exchange, 0)
    total = dup[pl.ds(0, half), :].astype(BF16).astype(F32)
    turned = pltpu.roll(total, rank, 1)
    dup[pl.ds(0, half), :] = jnp.where(low_lane, total, turned)
    dup[pl.ds(half, half), :] = jnp.where(low_lane, turned, total)

    def spread(t, _):
        p = pts[t]
        at = pl.ds(pl.multiple_of(t * seg, seg), seg)
        mine = dup[at, :]
        for b in range(blocks):
            e[at, b * LANES : (b + 1) * LANES] = jnp.where(turn_lane + 2 * b == p, mine, 0.0).astype(
                BF16
            )
        return 0

    lax.fori_loop(0, turns, spread, 0)

    def raise_chunk(c, _):
        delta[rows_of(c), :] = jnp.dot(
            e[rows_of(c), :], arecv[:, feats:], preferred_element_type=F32
        )
        return 0

    lax.fori_loop(0, chunks, raise_chunk, 0)

    def finish(c, _):
        acc[...] = part[i, rows_of(c)].astype(F32)

        @pl.when(i > 0)
        def _():
            arrival(0, i, c).wait_recv()
            acc[...] += rcv[0, i, rows_of(c)].astype(F32)

        @pl.when(i < n_t - 1)
        def _():
            arrival(1, i, c).wait_recv()
            acc[...] += rcv[1, i, rows_of(c)].astype(F32)

        keys_o[rows_of(c), :] = acc[:, :cols].astype(BF16)
        vals_o[rows_of(c), :] = (acc[:, cols:] + ADAPTER_SCALE * delta[rows_of(c), :]).astype(BF16)
        return 0

    lax.fori_loop(0, chunks, finish, 0)

    def sent(d, _):
        @pl.when(d != i)
        def _():
            def chunk(c, _):
                msg(d, c).wait_send()
                return 0

            lax.fori_loop(0, chunks, chunk, 0)

        return 0

    lax.fori_loop(0, n_t, sent, 0)

    def bank_sent(k, _):
        d = lax.rem(me + k, n_b)
        ids_msg(d, me).wait_send()
        adapter_msg(d, me).wait_send()
        return 0

    lax.fori_loop(1, n_b, bank_sent, 0)

    @pl.when(i < n_t - 1)
    def _():
        inner_msg(0).wait_send()

    @pl.when(i > 0)
    def _():
        inner_msg(1).wait_send()


def hand_over(keys_i, vals_i, keys_o, vals_o):
    keys_o[...] = keys_i[...]
    vals_o[...] = vals_i[...]


def shards(
    n_t,
    n_b,
    normed,
    turn_persona_ids,
    persona_bank_row,
    key_weight,
    value_weight,
    adapter_down_factor,
    adapter_up_factor,
):
    tokens, feats = normed.shape
    slots, rank, cols = adapter_up_factor.shape
    turns = turn_persona_ids.shape[0]
    step = tokens // 2
    chunks = tokens // step
    dma = pltpu.SemaphoreType.DMA
    any_space = pl.BlockSpec(memory_space=pl.ANY)
    smem = pl.BlockSpec(memory_space=pltpu.SMEM)
    vmem = pl.BlockSpec(memory_space=pltpu.VMEM)
    out = jax.ShapeDtypeStruct((tokens, cols), BF16)
    both = pl.pallas_call(
        functools.partial(kernel, n_t, n_b, step),
        out_shape=(out, out),
        in_specs=[smem, smem] + [any_space] * 5,
        out_specs=(vmem, vmem),
        scratch_shapes=[
            pltpu.VMEM((tokens, feats), BF16),
            pltpu.VMEM((n_t, feats, 2 * cols), BF16),
            pltpu.VMEM((slots, rank, feats), BF16),
            pltpu.VMEM((slots, rank, cols), BF16),
            pltpu.VMEM((n_t, tokens, 2 * cols), BF16),
            pltpu.VMEM((2, n_t, tokens, 2 * cols), BF16),
            pltpu.VMEM((n_b, 8, LANES), jnp.int32),
            pltpu.SMEM((n_b, 8, LANES), jnp.int32),
            pltpu.SMEM((turns,), jnp.int32),
            pltpu.VMEM((n_b * 2 * rank, feats + cols), BF16),
            pltpu.VMEM((n_b * 2 * rank, feats + cols), BF16),
            pltpu.VMEM((step, n_b * 2 * rank), F32),
            pltpu.VMEM((tokens, LANES), F32),
            pltpu.VMEM((tokens // 2, LANES), F32),
            pltpu.VMEM((2, tokens // 2, LANES), BF16),
            pltpu.VMEM((2, tokens // 2, LANES), BF16),
            pltpu.VMEM((tokens, n_b * 2 * rank), BF16),
            pltpu.VMEM((tokens, cols), F32),
            pltpu.VMEM((step, 2 * cols), F32),
            dma((chunks,)),
            dma((n_t, 2)),
            dma((2,)),
            dma((1,)),
            dma((n_b,)),
            dma((n_b,)),
            dma((n_b,)),
            dma((n_b,)),
            dma((n_t, chunks)),
            dma((2, n_t, chunks)),
            dma((2,)),
            dma((2,)),
        ],
        compiler_params=pltpu.CompilerParams(
            collective_id=0, has_side_effects=True, vmem_limit_bytes=58 * 1024 * 1024
        ),
        cost_estimate=pl.CostEstimate(
            flops=4 * tokens * feats * cols * n_t,
            bytes_accessed=2 * (tokens * feats + 2 * feats * cols * n_t + slots * rank * feats),
            transcendentals=0,
        ),
    )(
        turn_persona_ids,
        persona_bank_row,
        normed,
        key_weight,
        value_weight,
        adapter_down_factor,
        adapter_up_factor,
    )
    return pl.pallas_call(
        hand_over,
        out_shape=(out, out),
        in_specs=[vmem, vmem],
        out_specs=(vmem, vmem),
    )(*both)


def solution(mesh):
    placed = (
        P(("groups", "bank"), "tensor"),
        P(("groups", "bank")),
        P("groups"),
        P("tensor", None),
        P("tensor", None),
        P(("groups", "bank"), None, "tensor"),
        P(("groups", "bank"), None, "tensor"),
    )
    return jax.shard_map(
        functools.partial(shards, mesh.shape["tensor"], mesh.shape["bank"]),
        mesh=mesh,
        in_specs=placed,
        out_specs=(P(("groups", "bank"), "tensor"), P(("groups", "bank"), "tensor")),
        check_vma=False,
    )
```
